32 devices in a mesh: groups: 2 (over y), clus: 4 (over z), tp: 2 (over x), rep: 2 (over core).
Axes of the slice: x: 2, y: 2, z: 4, core: 2. Of those that a mesh axis runs over, the one named last changes fastest.
Arguments:
- hidden: bfloat16 [3072, 8192], P(('groups', 'clus'), ('tp', 'rep')), parts along dimension 0, may hold values from -6 to 6
- residual: bfloat16 [3072, 4096], P(('groups', 'clus'), ('tp', 'rep')), parts along dimension 0, may hold values from -6 to 6
- down_weight: bfloat16 [8192, 4096], P(('tp', 'rep'), 'clus'), may hold values from -0.0625 to 0.0625
- norm_gain: float32 [4096], P(('tp', 'rep')), may hold values from 0.1 to 1.9
- cluster_id: int32 [3072, 1], P(('groups', 'clus')), parts along dimension 0, may hold values from 0 to 23, as said below
Outputs:
- embedded: bfloat16 [3072, 4096], P(('groups', 'clus'), ('tp', 'rep')), parts along dimension 0
- score: float32 [3072], P(('groups', 'clus')), parts along dimension 0
The draws below stay inside these ranges and needn't reach their ends.
There are 2 independent parts, one for each index of `groups`. The reference program is written for one: setup_inputs(seed, part) draws one part's arguments, and reference() takes and returns one part's arrays. A program takes and returns all parts, laid end to end along the dimension named above; an argument that names none is the same for every part. Nothing has to cross between parts.
Inputs may be any that keep to these rules, and one draw needn't show every extreme that they name: `cluster_id`: the rows of one device name each cluster at most 32 times; one cluster is named exactly 32 times by the rows of every device.
All inputs are finite; a program needn't handle non-finite values.
Results may differ from the reference program's by a relative error of at most 0.0095.
Values may be sent and summed in bfloat16 or wider, within the bound.
No kernel may reach another device: no remote copies, remote signals or barrier semaphores. Data moves between devices by JAX's collectives and lax.ppermute only.
A program may use at most 128 MiB of HBM per device.

```python
import jax
import jax.numpy as jnp
from jax import lax

D = 4096
FFW = 8192
R_DEV = 384
ROWS = 1536
CLUSTERS = 24
CAP = 32
N_CLUS = 4
N_TP = 2
N_REP = 2


def shuffle_row(row_key, values):
    return jax.random.permutation(row_key, values)


def draw_cluster_id(key, part):
    key = jax.random.fold_in(key, 7)
    blocks = ROWS // R_DEV
    keys = jax.random.split(key, 7)
    limit = max(2, CLUSTERS // 8)
    standing = jax.random.permutation(keys[0], CLUSTERS).astype(jnp.int32)
    singles = jax.random.randint(keys[1], (), 1, limit + 1)
    doubles = jax.random.randint(keys[2], (), 1, limit + 1)
    is_full = standing == 0
    is_single = (standing >= 1) & (standing <= singles)
    is_double = (standing > singles) & (standing <= singles + doubles)
    popular = jax.random.randint(keys[3], (CLUSTERS,), 0, CAP + 1)
    homes = jax.random.randint(keys[4], (2, CLUSTERS), 0, blocks)
    block_index = jnp.arange(blocks, dtype=jnp.int32)[:, None, None]
    place = jnp.arange(CAP, dtype=jnp.int32)[None, None, :]
    first = (block_index == homes[0][None, :, None]) & (place == 0)
    second = (block_index == homes[1][None, :, None]) & (place == 1) & is_double[None, :, None]
    regular = 1 + (place < popular[None, :, None]).astype(jnp.int32)
    sparse = jnp.where(first | second, 3, 0)
    level = jnp.where(is_full[None, :, None], 3, jnp.where((is_single | is_double)[None, :, None], sparse, regular))
    noise = jax.random.randint(keys[5], (blocks, CLUSTERS, CAP), 0, 4096)
    slot_count = CLUSTERS * CAP
    position = jnp.arange(slot_count, dtype=jnp.int32).reshape(1, CLUSTERS, CAP)
    priority = ((level * 4096 + noise) * slot_count + position).reshape(blocks, slot_count)
    chosen = lax.top_k(priority, R_DEV)[1]
    labels = (chosen // CAP).astype(jnp.int32)
    row_keys = jax.random.split(keys[6], blocks)
    shuffled = jax.vmap(shuffle_row)(row_keys, labels)
    return shuffled.reshape(ROWS, 1).astype(jnp.int32)


def steps_of(key, shape, shards, least, high):
    level, own = 1.0, jax.random.fold_in(key, 6)
    for axis_at, blocks in shards:
        draws = jnp.exp(jax.random.uniform(jax.random.fold_in(own, axis_at), (blocks,), jnp.float32, least / len(shards), high / len(shards)))
        level = level * jnp.repeat(draws, shape[axis_at] // blocks).reshape([-1 if axis == axis_at else 1 for axis in range(len(shape))])
    return level


def normal_values(own_key, dims, scale, bound, cuts=(), held_as=jnp.bfloat16):
    drawn = jax.random.normal(own_key, dims, jnp.float32) * scale
    if len(cuts) > 0:
        drawn = steps_of(own_key, dims, cuts, -0.22, 0.18) * drawn
    return jnp.clip(drawn, min=-bound, max=bound).astype(held_as)


def setup_inputs(seed: int = 0, part: int = 0) -> dict:
    streams_of = jax.random.split(jax.random.key(seed), 6)
    part_keys = jax.random.split(jax.random.fold_in(streams_of[5], part), 6)
    return {
        "hidden": normal_values(part_keys[0], (ROWS, FFW), 1.0, 6.0, ((0, 4), (1, 4))),
        "residual": normal_values(part_keys[1], (ROWS, D), 1.0, 6.0, ((0, 4), (1, 4))),
        "down_weight": normal_values(streams_of[2], (FFW, D), FFW ** -0.5, 0.0625, ((0, 4), (1, 4))),
        "norm_gain": jnp.clip(1.0 + 0.18 * jax.random.normal(streams_of[3], (D,), jnp.float32), 0.1, 1.9),
        "cluster_id": draw_cluster_id(jax.random.fold_in(jax.random.fold_in(streams_of[5], part), 71), part),
    }


EPS = 1e-06

def reference(hidden, residual, down_weight, norm_gain, cluster_id):
    splits = N_TP * N_REP
    block_width = FFW // splits

    def add_share(which, accum):
        begin = (which * block_width).astype(jnp.int32)
        hidden_part = lax.dynamic_slice_in_dim(hidden, begin, block_width, 1)
        weight_part = lax.dynamic_slice_in_dim(down_weight, begin, block_width, 0)
        share = jnp.dot(hidden_part, weight_part, preferred_element_type=jnp.float32).astype(jnp.bfloat16)
        share = lax.optimization_barrier(share)
        return accum + share.astype(jnp.float32)
    mixed = lax.fori_loop(0, splits, add_share, residual.astype(jnp.float32))
    scaled = mixed * norm_gain[None, :]
    total = lax.optimization_barrier(jnp.sum(scaled * scaled, axis=1))
    embedded = (scaled * lax.rsqrt(total + EPS)[:, None]).astype(jnp.bfloat16)
    labels = cluster_id[:, 0].astype(jnp.int32)
    order = jnp.argsort(labels, stable=True).astype(jnp.int32)
    counts = lax.optimization_barrier(jnp.sum((labels[:, None] == jnp.arange(CLUSTERS, dtype=jnp.int32)[None, :]).astype(jnp.int32), axis=0)).astype(jnp.int32)
    starts = (jnp.cumsum(counts) - counts).astype(jnp.int32)
    span = N_CLUS * CAP
    ordered = jnp.concatenate([embedded[order], jnp.zeros((span, D), jnp.bfloat16)], axis=0)
    index = jnp.arange(span, dtype=jnp.int32)

    def one_cluster(which):
        block = lax.dynamic_slice_in_dim(ordered, starts[which], span, 0)
        gram = lax.dot_general(block, block, (((1,), (1,)), ((), ())), preferred_element_type=jnp.float32)
        keep = (index[None, :] < counts[which]) & (index[:, None] != index[None, :])
        best = lax.optimization_barrier(jnp.max(jnp.where(keep, gram, jnp.float32(-4.0)), axis=1))
        found = jnp.any(keep, axis=1)
        return jnp.where(found, D ** 0.5 * best, jnp.float32(-1.0))
    table = lax.map(one_cluster, jnp.arange(CLUSTERS, dtype=jnp.int32))
    sorted_labels = labels[order]
    within = (jnp.arange(ROWS, dtype=jnp.int32) - starts[sorted_labels]).astype(jnp.int32)
    sorted_score = table[sorted_labels, within]
    score = jnp.zeros((ROWS,), jnp.float32).at[order].set(sorted_score)
    return (embedded, score)
```

```python
import jax
import jax.numpy as jnp
from jax import lax
from jax.sharding import PartitionSpec as P

D = 4096
CL_OWN = 6
EPS = 1e-06
F32, BF16 = jnp.float32, jnp.bfloat16


def best_match(block, valid):
    slots = block.shape[2]
    row_index = jnp.arange(block.shape[1], dtype=jnp.int32)
    col_index = jnp.arange(slots, dtype=jnp.int32)
    keep = valid[:, None, :] & (row_index[:, None] != col_index[None, :])[None, :, :]
    best = jnp.max(jnp.where(keep, block, jnp.float32(-4.0)), axis=2)
    found = jnp.any(keep, axis=2)
    return jnp.where(found, D**0.5 * best, jnp.float32(-1.0))


def any_mesh(hidden, residual, down_weight, norm_gain, cluster_id):
    rows = hidden.shape[0]
    owners = lax.axis_size("clus")
    per_owner = CL_OWN
    clusters = per_owner * owners
    capacity = 2 * rows // clusters
    span = owners * capacity
    terms = jnp.dot(
        hidden,
        lax.all_gather(down_weight, "clus", axis=1, tiled=True),
        preferred_element_type=jnp.float32,
    )
    summed = lax.psum_scatter(
        terms.astype(jnp.bfloat16), ("tp", "rep"), scatter_dimension=1, tiled=True
    ).astype(jnp.float32)
    scaled = (summed + residual.astype(jnp.float32)) * norm_gain[None, :]
    total = lax.psum(jnp.sum(scaled * scaled, axis=1), ("tp", "rep"))
    embedded = (scaled * lax.rsqrt(total + EPS)[:, None]).astype(jnp.bfloat16)
    labels = cluster_id[:, 0]
    owner = labels // per_owner
    local = labels % per_owner
    positions = jnp.arange(rows, dtype=jnp.int32)
    earlier = (labels[:, None] == labels[None, :]) & (positions[None, :] < positions[:, None])
    rank = jnp.sum(earlier.astype(jnp.int32), axis=1)
    target = local * span + owner * capacity + rank
    placing = jnp.arange(per_owner * span, dtype=jnp.int32)[:, None] == target[None, :]
    outgoing = jnp.dot(
        placing.astype(jnp.bfloat16), embedded, preferred_element_type=jnp.float32
    ).astype(jnp.bfloat16)
    outgoing = outgoing.reshape(per_owner, span, embedded.shape[1])
    present = (
        jnp.sum(placing.astype(jnp.float32), axis=1).astype(jnp.bfloat16).reshape(per_owner, span)
    )
    arrived, filled = (
        lax.all_to_all(outgoing, "clus", split_axis=1, concat_axis=1, tiled=True),
        lax.all_to_all(present, "clus", split_axis=1, concat_axis=1, tiled=True),
    )
    partial_value = jnp.einsum("ksd,ktd->kst", arrived, arrived, preferred_element_type=jnp.float32)
    valid = filled > 0
    gram = lax.psum(partial_value.astype(jnp.bfloat16), ("tp", "rep")).astype(jnp.float32)
    best = best_match(gram, valid)
    returned = lax.all_to_all(best, "clus", split_axis=1, concat_axis=1, tiled=True)
    score = jnp.sum(jnp.where(placing, returned.reshape(-1)[:, None], jnp.float32(0.0)), axis=0)
    return (embedded, score)


OUT_IN = [(0, 1), (3, 2)]
IN_OUT = [(1, 0), (2, 3)]
IN_IN = [(1, 2), (2, 1)]
FAR_IN = [(0, 2), (3, 1)]
SWAP = [(0, 1), (1, 0)]
CHUNKS = 4


def after(value, *earlier):
    return lax.optimization_barrier((value, *earlier))[0]


def zc(pairs):
    return [(a * 2 + b, c * 2 + d) for (a, b), (c, d) in pairs]


def line_of_four(hidden, residual, down_weight, norm_gain, cluster_id):
    rows, depth = hidden.shape
    cols = down_weight.shape[1]
    half = cols // 2
    q = half // CHUNKS
    every = 4 * rows
    y, z, x, c = (lax.axis_index(a) for a in ("groups", "clus", "tp", "rep"))
    side = z // 2
    inner = (z == 1) | (z == 2)

    mine = cluster_id[:, 0]
    from_back = [
        lax.ppermute(mine, "clus", [(i, (i + k) % 4) for i in range(4)]) for k in (1, 2, 3)
    ]
    order = jnp.arange(every, dtype=jnp.int32)
    ids = [(z + 4 - k) % 4 * rows + order[:rows] for k in range(4)]

    def arranged_here(v):
        return jnp.concatenate(
            [v[0], jnp.where(side == 0, v[1], v[3]), jnp.where(side == 0, v[3], v[1]), v[2]]
        )

    labels = arranged_here([mine, *from_back])
    ids = arranged_here(ids)
    before = (labels[None, :] < labels[:, None]) | (
        (labels[None, :] == labels[:, None]) & (ids[None, :] < ids[:, None])
    )
    place = jnp.sum(before.astype(jnp.int32), axis=1)
    at_place = order[:, None] == place[None, :]
    placing = at_place.astype(BF16)
    sorted_labels = jnp.sum(jnp.where(at_place, labels[None, :], 0), axis=1)

    h_outer = lax.ppermute(hidden, "clus", OUT_IN)
    h_other = lax.ppermute(hidden, "clus", IN_IN)
    h_far = lax.ppermute(h_outer, "clus", IN_IN)
    blocks = [hidden, h_outer, h_other, h_far]

    mine = lax.dynamic_slice_in_dim(residual, x * half, half, 1)
    theirs = lax.dynamic_slice_in_dim(residual, (1 - x) * half, half, 1)
    came = lax.ppermute(theirs, "tp", SWAP)
    near_side = jnp.where(side == x, mine, came)
    far_side = jnp.where(side == x, came, mine)

    w_half = lax.dynamic_slice_in_dim(down_weight, y * (depth // 2), depth // 2, 0)
    w_chunks = []
    sent = [h_outer, h_outer]
    res_far = res_near = None
    for j in range(CHUNKS):
        piece = jnp.concatenate(
            [w_half[:, j * q : (j + 1) * q], w_half[:, half + j * q : half + (j + 1) * q]], axis=1
        )
        got = lax.ppermute(after(piece, sent[-2]), "clus", OUT_IN)
        sent.append(got)
        if j == 0:
            res_far = lax.ppermute(after(far_side, sent[-2]), "clus", FAR_IN)
            sent.append(res_far)
        if j == 2:
            res_near = lax.ppermute(after(near_side, sent[-2]), "clus", OUT_IN)
            sent.append(res_near)
        other = lax.ppermute(got, "groups", SWAP)
        w_chunks.append(
            jnp.where(
                y == 0,
                jnp.concatenate([got, other], axis=0),
                jnp.concatenate([other, got], axis=0),
            )
        )
    res_other = lax.ppermute(after(far_side, h_other), "clus", IN_IN)
    res = jnp.concatenate([near_side, res_near, res_other, res_far], axis=0).astype(F32)

    gain_other = lax.ppermute(norm_gain, "tp", SWAP)
    gain_late = jnp.where(x == c, norm_gain, gain_other)
    gain_early = jnp.where(x == c, gain_other, norm_gain)
    gain_late = lax.dynamic_slice_in_dim(gain_late, x * half, half, 0)[None, :]
    gain_early = lax.dynamic_slice_in_dim(gain_early, x * half, half, 0)[None, :]

    def summed(part, core_pairs, x_pairs, width):
        met = lax.ppermute(part, ("clus", "rep"), core_pairs)
        both = part.astype(F32) + met.astype(F32)
        keep = lax.dynamic_slice_in_dim(both, x * width, width, 1)
        give = lax.dynamic_slice_in_dim(both, (1 - x) * width, width, 1).astype(BF16)
        return keep + lax.ppermute(give, ("clus", "tp", "rep"), x_pairs).astype(F32)

    early_core = zc([((1, 0), (1, 1)), ((2, 1), (2, 0))])
    late_core = zc([((1, 1), (1, 0)), ((2, 0), (2, 1))])
    early_x = [(5, 7), (7, 5), (8, 10), (10, 8)]
    late_x = [(4, 6), (6, 4), (9, 11), (11, 9)]

    early = []
    for block in blocks:
        part = jnp.dot(block, down_weight, preferred_element_type=F32).astype(BF16)
        early.append(summed(part, early_core, early_x, half))
    early = ((jnp.concatenate(early, axis=0) + res) * gain_early).astype(BF16)

    late = []
    for w in w_chunks:
        part = jnp.concatenate(
            [jnp.dot(block, w, preferred_element_type=F32).astype(BF16) for block in blocks], axis=0
        )
        late.append(summed(part, late_core, late_x, q))
    late = ((jnp.concatenate(late, axis=1) + res) * gain_late).astype(BF16)

    def home(value, near, other, far, where):
        value = value.reshape(4, rows, half)
        moved = (
            lax.ppermute(value[1], ("clus", "rep"), zc(near))
            + lax.ppermute(value[2], ("clus", "rep"), zc(other))
            + lax.ppermute(value[3], ("clus", "rep"), zc(far))
        )
        return jnp.where(z == where, value[0], moved)

    early_rows = home(
        early,
        [((2, 0), (3, 0)), ((1, 1), (0, 1))],
        [((2, 0), (1, 0)), ((1, 1), (2, 1))],
        [((2, 0), (0, 0)), ((1, 1), (3, 1))],
        2 - c,
    )
    late_rows = home(
        late,
        [((1, 0), (0, 0)), ((2, 1), (3, 1))],
        [((1, 0), (2, 0)), ((2, 1), (1, 1))],
        [((1, 0), (3, 0)), ((2, 1), (0, 1))],
        1 + c,
    )
    kept = jnp.where(x == c, late_rows, early_rows)
    came = lax.ppermute(late_rows, ("tp", "rep"), [(2, 0), (1, 3)]) + lax.ppermute(
        early_rows, ("tp", "rep"), [(0, 2), (3, 1)]
    )
    unscaled = jnp.where(
        x == 0, jnp.concatenate([kept, came], axis=1), jnp.concatenate([came, kept], axis=1)
    )

    tile = 128
    tiles = every // tile
    values = jnp.where(z == 1 + c, late, early)
    arranged = jnp.dot(placing, values, preferred_element_type=F32).astype(BF16)
    squares = jnp.sum(jnp.square(arranged.astype(F32)), axis=1)
    stacked = arranged.reshape(tiles, tile, half)
    following = jnp.concatenate([stacked[1:], jnp.zeros_like(stacked[:1])], axis=0)
    gram = jnp.einsum(
        "tad,tbd->tab",
        stacked,
        jnp.concatenate([stacked, following], axis=1),
        preferred_element_type=F32,
    ).astype(BF16)

    def share(value, axis, index):
        n = value.shape[0] // 2
        give = lax.dynamic_slice_in_dim(value, (1 - index) * n, n, 0)
        keep = lax.dynamic_slice_in_dim(value, index * n, n, 0)
        met = lax.ppermute(give.astype(BF16), axis, SWAP)
        return keep.astype(F32) + met.astype(F32)

    gram = share(share(gram, "rep", c), "tp", x).astype(BF16)
    gram = gram.astype(F32) + lax.ppermute(gram, "clus", IN_IN).astype(F32)
    total = squares + lax.ppermute(squares, "rep", SWAP)
    total = total + lax.ppermute(total, "tp", SWAP)
    total = total + lax.ppermute(total, "clus", IN_IN)

    n = tiles // 4
    first = (2 * c + x) * n
    pad = lambda a, v: jnp.concatenate([a, jnp.full((tile,), v, a.dtype)]).reshape(tiles + 1, tile)
    span = lambda a: lax.dynamic_slice_in_dim(a, first, n + 1, 0)
    both = lambda a: jnp.concatenate([a[:-1], a[1:]], axis=1)
    scale = span(pad(lax.rsqrt(total + EPS), 0.0))
    names = span(pad(sorted_labels, -1))
    sims = gram * scale[:-1, :, None] * both(scale)[:, None, :]
    at = jnp.arange(tile, dtype=jnp.int32)[:, None] != jnp.arange(2 * tile, dtype=jnp.int32)[None, :]
    keep = (names[:-1, :, None] == both(names)[:, None, :]) & at[None]
    sims = jnp.where(keep, sims, F32(-4.0))
    found = jnp.stack([jnp.max(sims, axis=2), jnp.max(sims[:, :, tile:], axis=1)])
    for axis, index in (("tp", x), ("rep", c)):
        met = lax.ppermute(found, axis, SWAP)
        found = jnp.where(
            index == 0, jnp.concatenate([found, met], axis=1), jnp.concatenate([met, found], axis=1)
        )
    shifted = jnp.concatenate([jnp.full((1, tile), -4.0, F32), found[1, :-1]], axis=0)
    best = jnp.maximum(found[0], shifted).reshape(every)

    best = jnp.where(inner, best, lax.ppermute(best, "clus", IN_OUT))
    total = jnp.where(inner, total, lax.ppermute(total, "clus", IN_OUT))
    chosen = place[:rows, None] == order[None, :]
    best = jnp.sum(jnp.where(chosen, best[None, :], 0.0), axis=1)
    total = jnp.sum(jnp.where(chosen, total[None, :], 0.0), axis=1)
    score = jnp.where(best > -2.0, D**0.5 * best, F32(-1.0))
    embedded = (unscaled.astype(F32) * lax.rsqrt(total + EPS)[:, None]).astype(BF16)
    return (embedded, score)


def solution(mesh):
    size = mesh.shape
    four = size["clus"] == 4 and size["groups"] == size["tp"] == size["rep"] == 2
    return jax.shard_map(
        line_of_four if four else any_mesh,
        mesh=mesh,
        in_specs=(
            P(("groups", "clus"), ("tp", "rep")),
            P(("groups", "clus"), ("tp", "rep")),
            P(("tp", "rep"), "clus"),
            P(("tp", "rep")),
            P(("groups", "clus"), None),
        ),
        out_specs=(P(("groups", "clus"), ("tp", "rep")), P(("groups", "clus"))),
        check_vma=False,
    )
```

```python
import jax
import jax.numpy as jnp
from jax import lax
from jax.experimental import pallas as pl
from jax.experimental.pallas import tpu as pltpu
from jax.sharding import PartitionSpec as P

D = 4096
CL_OWN = 6
EPS = 1e-06
F32, BF16 = jnp.float32, jnp.bfloat16


def best_match(block, valid):
    slots = block.shape[2]
    row_index = jnp.arange(block.shape[1], dtype=jnp.int32)
    col_index = jnp.arange(slots, dtype=jnp.int32)
    keep = valid[:, None, :] & (row_index[:, None] != col_index[None, :])[None, :, :]
    best = jnp.max(jnp.where(keep, block, jnp.float32(-4.0)), axis=2)
    found = jnp.any(keep, axis=2)
    return jnp.where(found, D**0.5 * best, jnp.float32(-1.0))


def any_mesh(hidden, residual, down_weight, norm_gain, cluster_id):
    rows = hidden.shape[0]
    owners = lax.axis_size("clus")
    per_owner = CL_OWN
    clusters = per_owner * owners
    capacity = 2 * rows // clusters
    span = owners * capacity
    terms = jnp.dot(
        hidden,
        lax.all_gather(down_weight, "clus", axis=1, tiled=True),
        preferred_element_type=jnp.float32,
    )
    summed = lax.psum_scatter(
        terms.astype(jnp.bfloat16), ("tp", "rep"), scatter_dimension=1, tiled=True
    ).astype(jnp.float32)
    scaled = (summed + residual.astype(jnp.float32)) * norm_gain[None, :]
    total = lax.psum(jnp.sum(scaled * scaled, axis=1), ("tp", "rep"))
    embedded = (scaled * lax.rsqrt(total + EPS)[:, None]).astype(jnp.bfloat16)
    labels = cluster_id[:, 0]
    owner = labels // per_owner
    local = labels % per_owner
    positions = jnp.arange(rows, dtype=jnp.int32)
    earlier = (labels[:, None] == labels[None, :]) & (positions[None, :] < positions[:, None])
    rank = jnp.sum(earlier.astype(jnp.int32), axis=1)
    target = local * span + owner * capacity + rank
    placing = jnp.arange(per_owner * span, dtype=jnp.int32)[:, None] == target[None, :]
    outgoing = jnp.dot(
        placing.astype(jnp.bfloat16), embedded, preferred_element_type=jnp.float32
    ).astype(jnp.bfloat16)
    outgoing = outgoing.reshape(per_owner, span, embedded.shape[1])
    present = (
        jnp.sum(placing.astype(jnp.float32), axis=1).astype(jnp.bfloat16).reshape(per_owner, span)
    )
    arrived, filled = (
        lax.all_to_all(outgoing, "clus", split_axis=1, concat_axis=1, tiled=True),
        lax.all_to_all(present, "clus", split_axis=1, concat_axis=1, tiled=True),
    )
    partial_value = jnp.einsum("ksd,ktd->kst", arrived, arrived, preferred_element_type=jnp.float32)
    valid = filled > 0
    gram = lax.psum(partial_value.astype(jnp.bfloat16), ("tp", "rep")).astype(jnp.float32)
    best = best_match(gram, valid)
    returned = lax.all_to_all(best, "clus", split_axis=1, concat_axis=1, tiled=True)
    score = jnp.sum(jnp.where(placing, returned.reshape(-1)[:, None], jnp.float32(0.0)), axis=0)
    return (embedded, score)


OUT_IN = [(0, 1), (3, 2)]
IN_OUT = [(1, 0), (2, 3)]
IN_IN = [(1, 2), (2, 1)]
FAR_IN = [(0, 2), (3, 1)]
SWAP = [(0, 1), (1, 0)]
CHUNKS = 4


def after(value, *earlier):
    return lax.optimization_barrier((value, *earlier))[0] if earlier else value


def zc(pairs):
    return [(a * 2 + b, c * 2 + d) for (a, b), (c, d) in pairs]


FREE = pl.CostEstimate(flops=1024, bytes_accessed=1024, transcendentals=0)


def late_part(y, rows, own, other, which=0):
    every, depth = rows.shape
    cols = other.shape[1]
    block = every // 2

    def body(_, a, b, own, other, out):
        total = jnp.dot(a[...], own[...], preferred_element_type=F32)
        total = total + jnp.dot(b[...], other[...], preferred_element_type=F32)
        out[...] = total.astype(BF16)

    return pl.pallas_call(
        body,
        grid_spec=pltpu.PrefetchScalarGridSpec(
            num_scalar_prefetch=1,
            grid=(every // block,),
            in_specs=[
                pl.BlockSpec((block, depth // 2), lambda i, y: (i, y[0])),
                pl.BlockSpec((block, depth // 2), lambda i, y: (i, 1 - y[0])),
                pl.BlockSpec((depth // 2, cols), lambda i, y: (0, which)),
                pl.BlockSpec((depth // 2, cols), lambda i, y: (0, 0)),
            ],
            out_specs=pl.BlockSpec((block, cols), lambda i, y: (i, 0)),
        ),
        out_shape=jax.ShapeDtypeStruct((every, cols), BF16),
        compiler_params=pltpu.CompilerParams(vmem_limit_bytes=24 * 2**20),
        cost_estimate=FREE,
        name="late_part",
    )(jnp.asarray(y, jnp.int32).reshape(1), rows, rows, own, other)


def product(rows, w):
    m, depth = rows.shape
    cols = w.shape[1]
    block = 256

    def body(a, b, out):
        out[...] = jnp.dot(a[...], b[...], preferred_element_type=F32).astype(BF16)

    return pl.pallas_call(
        body,
        grid=(cols // block,),
        in_specs=[
            pl.BlockSpec((m, depth), lambda i: (0, 0)),
            pl.BlockSpec((depth, block), lambda i: (0, i)),
        ],
        out_specs=pl.BlockSpec((m, block), lambda i: (0, i)),
        out_shape=jax.ShapeDtypeStruct((m, cols), BF16),
        compiler_params=pltpu.CompilerParams(vmem_limit_bytes=24 * 2**20),
        cost_estimate=FREE,
        name="product",
    )(rows, w)


def fold(x, part, met):
    rows, cols = part.shape
    width = cols // 2
    block = 384

    def body(_, a, b, c, d, keep, give):
        keep[...] = a[...].astype(F32) + b[...].astype(F32)
        give[...] = (c[...].astype(F32) + d[...].astype(F32)).astype(BF16)

    kept = pl.BlockSpec((block, width), lambda i, x: (i, x[0]))
    given = pl.BlockSpec((block, width), lambda i, x: (i, 1 - x[0]))
    out = pl.BlockSpec((block, width), lambda i, x: (i, 0))
    return pl.pallas_call(
        body,
        grid_spec=pltpu.PrefetchScalarGridSpec(
            num_scalar_prefetch=1,
            grid=(rows // block,),
            in_specs=[kept, kept, given, given],
            out_specs=[out, out],
        ),
        out_shape=[
            jax.ShapeDtypeStruct((rows, width), F32),
            jax.ShapeDtypeStruct((rows, width), BF16),
        ],
        compiler_params=pltpu.CompilerParams(vmem_limit_bytes=24 * 2**20),
        cost_estimate=FREE,
        name="fold",
    )(jnp.asarray(x, jnp.int32).reshape(1), part, met, part, met)


def tile_gram(is_late, place, late, early):
    every, width = late.shape
    tile = 128
    tiles = every // tile

    def body(flag, place, late, early, gram, squares, rows):
        rows[every:, :] = jnp.zeros((tile, width), BF16)
        value = jnp.where(flag[0] == 1, late[...], early[...])
        at = jax.lax.broadcasted_iota(jnp.int32, (tile, every), 0)
        for t in range(tiles):
            one = (at + t * tile == place[...]).astype(F32).astype(BF16)
            rows[t * tile : (t + 1) * tile, :] = jnp.dot(
                one, value, preferred_element_type=F32
            ).astype(BF16)
        i = jax.lax.broadcasted_iota(jnp.int32, (tile, tile), 0)
        j = jax.lax.broadcasted_iota(jnp.int32, (tile, tile), 1)
        for t in range(tiles):
            product = jax.lax.dot_general(
                rows[t * tile : (t + 1) * tile, :],
                rows[t * tile : (t + 2) * tile, :],
                (((1,), (1,)), ((), ())),
                preferred_element_type=F32,
            )
            gram[t] = product.astype(BF16)
            squares[t : t + 1, :] = jnp.sum(
                jnp.where(i == j, product[:, :tile], 0.0), axis=0, keepdims=True
            )

    return pl.pallas_call(
        body,
        grid_spec=pltpu.PrefetchScalarGridSpec(
            num_scalar_prefetch=1,
            grid=(1,),
            in_specs=[
                pl.BlockSpec((1, every), lambda i, f: (0, 0)),
                pl.BlockSpec((every, width), lambda i, f: (0, 0)),
                pl.BlockSpec((every, width), lambda i, f: (0, 0)),
            ],
            out_specs=[
                pl.BlockSpec((tiles, tile, 2 * tile), lambda i, f: (0, 0, 0)),
                pl.BlockSpec((tiles, tile), lambda i, f: (0, 0)),
            ],
            scratch_shapes=[pltpu.VMEM((every + tile, width), BF16)],
        ),
        out_shape=[
            jax.ShapeDtypeStruct((tiles, tile, 2 * tile), BF16),
            jax.ShapeDtypeStruct((tiles, tile), F32),
        ],
        compiler_params=pltpu.CompilerParams(vmem_limit_bytes=24 * 2**20),
        cost_estimate=FREE,
        name="tile_gram",
    )(jnp.asarray(is_late, jnp.int32).reshape(1), place.reshape(1, every), late, early)


def line_of_four(hidden, residual, down_weight, norm_gain, cluster_id):
    rows, depth = hidden.shape
    cols = down_weight.shape[1]
    half = cols // 2
    q = half // CHUNKS
    every = 4 * rows
    y, z, x, c = (lax.axis_index(a) for a in ("groups", "clus", "tp", "rep"))
    side = z // 2
    inner = (z == 1) | (z == 2)

    early_core = zc([((1, 0), (1, 1)), ((2, 1), (2, 0))])
    late_core = zc([((1, 1), (1, 0)), ((2, 0), (2, 1))])
    early_x = [(5, 7), (7, 5), (8, 10), (10, 8)]
    late_x = [(4, 6), (6, 4), (9, 11), (11, 9)]

    def over_rep(part, pairs):
        return fold(x, part, lax.ppermute(part, ("clus", "rep"), pairs))

    def over_tp(keep, give, pairs):
        return keep + lax.ppermute(give, ("clus", "tp", "rep"), pairs).astype(F32)

    def across(value, *gates):
        return lax.ppermute(after(value, *gates), "groups", SWAP)

    def inward(value, *gates):
        return lax.ppermute(after(value, *gates), "clus", OUT_IN)

    stage = lax.optimization_barrier
    names = cluster_id[:, 0]
    h_outer = inward(hidden)
    h_other = lax.ppermute(hidden, "clus", IN_IN)
    names = jnp.concatenate(
        [names] + [lax.ppermute(names, "clus", pairs) for pairs in (OUT_IN, IN_IN, FAR_IN)]
    )
    mine = lax.dynamic_slice_in_dim(residual, x * half, half, 1)
    theirs = lax.dynamic_slice_in_dim(residual, (1 - x) * half, half, 1)
    w_half = lax.dynamic_slice_in_dim(down_weight, y * (depth // 2), depth // 2, 0)
    taken = lambda j, n: [w_half[:, i * half + j * q : i * half + (j + n) * q] for i in range(2)]
    pieces = [jnp.concatenate(v, axis=1) for v in (taken(0, 2), taken(2, 2))]
    part = product(hidden, down_weight)

    h_outer, h_other, names, part, pieces, theirs = stage(
        (h_outer, h_other, names, part, pieces, theirs)
    )
    got0 = inward(pieces[0])
    top = rows // 2
    far0 = lax.ppermute(h_outer[:top], "clus", IN_IN)
    came = lax.ppermute(theirs, "tp", SWAP)
    gain_other = lax.ppermute(norm_gain, "tp", SWAP)
    first = []
    part = [part] + [product(after(v, came), down_weight) for v in (h_outer, h_other)]
    first += [over_rep(v, early_core) for v in part]

    got0, pieces, came, gain_other, part, names, far0, first = stage(
        (got0, pieces, came, gain_other, part, names, far0, first)
    )
    far1 = lax.ppermute(h_outer[top:], "clus", IN_IN)
    got1 = inward(pieces[1])
    other0 = across(got0)
    order = jnp.arange(every, dtype=jnp.int32)
    planes = jnp.where(side == 0, jnp.array([1, 0, 2, 3]), jnp.array([2, 3, 1, 0]))
    ids = (planes[:, None] * rows + order[None, :rows]).reshape(every)
    before = (names[None, :] < names[:, None]) | (
        (names[None, :] == names[:, None]) & (ids[None, :] < ids[:, None])
    )
    place = jnp.sum(before.astype(jnp.int32), axis=1)
    at_place = order[:, None] == place[None, :]
    sorted_labels = jnp.sum(jnp.where(at_place, names[None, :], 0), axis=1)
    near_side = jnp.where(side == x, mine, came)
    far_side = jnp.where(side == x, came, mine)

    got1, other0, far0, far1, place, sorted_labels, first, near_side, far_side = stage(
        (got1, other0, far0, far1, place, sorted_labels, first, near_side, far_side)
    )
    far = jnp.concatenate([far0, far1], axis=0)
    other1 = across(got1)
    stack = jnp.concatenate([hidden, h_outer, h_other, far], axis=0)
    late0 = late_part(y, stack, got0, other0)
    res_near = inward(near_side)
    res_far = lax.ppermute(far_side, "clus", FAR_IN)
    res_other = lax.ppermute(after(far_side, late0), "clus", IN_IN)
    res = jnp.concatenate([near_side, res_near, res_other, res_far], axis=0).astype(F32)
    first = over_tp(*(jnp.concatenate(v, axis=0) for v in zip(*first)), early_x)
    last = over_rep(product(after(far, late0), down_weight), early_core)
    sum0 = over_rep(late0, late_core)
    late1 = late_part(y, after(stack, *last), got1, other1)
    last = over_tp(*last, early_x)
    sum0 = over_tp(*sum0, late_x)
    sum1 = over_tp(*over_rep(late1, late_core), late_x)
    early = jnp.concatenate([first, last], axis=0)

    gain_late = jnp.where(x == c, norm_gain, gain_other)
    gain_early = jnp.where(x == c, gain_other, norm_gain)
    gain_late = lax.dynamic_slice_in_dim(gain_late, x * half, half, 0)[None, :]
    gain_early = lax.dynamic_slice_in_dim(gain_early, x * half, half, 0)[None, :]
    early = ((early + res) * gain_early).astype(BF16)
    def home(value, near, other, far, where):
        value = value.reshape(4, rows, half)
        moved = (
            lax.ppermute(value[1], ("clus", "rep"), zc(near))
            + lax.ppermute(value[2], ("clus", "rep"), zc(other))
            + lax.ppermute(value[3], ("clus", "rep"), zc(far))
        )
        return jnp.where(z == where, value[0], moved)

    early_rows = home(
        early,
        [((2, 0), (3, 0)), ((1, 1), (0, 1))],
        [((2, 0), (1, 0)), ((1, 1), (2, 1))],
        [((2, 0), (0, 0)), ((1, 1), (3, 1))],
        2 - c,
    )
    sum1 = after(sum1, early_rows)
    late = [
        ((v + res[:, j * q : k * q]) * gain_late[:, j * q : k * q]).astype(BF16)
        for v, j, k in ((sum0, 0, 2), (sum1, 2, 4))
    ]
    late = jnp.concatenate(late, axis=1)

    tile = 128
    tiles = every // tile
    gram, squares = tile_gram(z == 1 + c, place, late, early)
    gram = gram.reshape(every, 2 * tile)
    squares = squares.reshape(tiles // 2, 2 * tile)
    spare = -tiles % 16

    def pack(gram, squares):
        high = lax.reduce_precision(squares, 8, 7)
        ends = jnp.zeros((spare, 2 * tile), BF16)
        return jnp.concatenate(
            [gram.astype(BF16), high.astype(BF16), (squares - high).astype(BF16), ends], axis=0
        )

    def meet(gram, squares, met):
        n = gram.shape[0]
        ends = met[n : n + tiles].astype(F32)
        return (
            gram.astype(F32) + met[:n].astype(F32),
            squares + ends[: tiles // 2] + ends[tiles // 2 :],
        )

    for axis, index in (("rep", c), ("tp", x)):
        n = gram.shape[0] // 2
        give = lax.dynamic_slice_in_dim(gram, (1 - index) * n, n, 0)
        keep = lax.dynamic_slice_in_dim(gram, index * n, n, 0)
        gram, squares = meet(keep, squares, lax.ppermute(pack(give, squares), axis, SWAP))
    late_rows = home(
        late,
        [((1, 0), (0, 0)), ((2, 1), (3, 1))],
        [((1, 0), (2, 0)), ((2, 1), (1, 1))],
        [((1, 0), (3, 0)), ((2, 1), (0, 1))],
        1 + c,
    )
    kept = jnp.where(x == c, late_rows, early_rows)
    came = lax.ppermute(late_rows, ("tp", "rep"), [(2, 0), (1, 3)]) + lax.ppermute(
        early_rows, ("tp", "rep"), [(0, 2), (3, 1)]
    )
    unscaled = jnp.where(
        x == 0, jnp.concatenate([kept, came], axis=1), jnp.concatenate([came, kept], axis=1)
    )

    gram = after(gram, late_rows)
    gram = gram.astype(BF16)
    gram, squares = meet(gram, squares, lax.ppermute(pack(gram, squares), "clus", IN_IN))
    gram = gram.reshape(-1, tile, 2 * tile)
    total = squares.reshape(every)

    n = tiles // 4
    first = (2 * c + x) * n
    pad = lambda a, v: jnp.concatenate([a, jnp.full((tile,), v, a.dtype)]).reshape(tiles + 1, tile)
    span = lambda a: lax.dynamic_slice_in_dim(a, first, n + 1, 0)
    both = lambda a: jnp.concatenate([a[:-1], a[1:]], axis=1)
    scale = span(pad(lax.rsqrt(total + EPS), 0.0))
    tags = span(pad(sorted_labels, -1))
    sims = gram * scale[:-1, :, None] * both(scale)[:, None, :]
    at = jnp.arange(tile, dtype=jnp.int32)[:, None] != jnp.arange(2 * tile, dtype=jnp.int32)[None, :]
    keep = (tags[:-1, :, None] == both(tags)[:, None, :]) & at[None]
    sims = jnp.where(keep, sims, F32(-4.0))
    found = jnp.stack([jnp.max(sims, axis=2), jnp.max(sims[:, :, tile:], axis=1)])
    found = after(found, came)
    for axis, index in (("tp", x), ("rep", c)):
        met = lax.ppermute(found, axis, SWAP)
        found = jnp.where(
            index == 0, jnp.concatenate([found, met], axis=1), jnp.concatenate([met, found], axis=1)
        )
    shifted = jnp.concatenate([jnp.full((1, tile), -4.0, F32), found[1, :-1]], axis=0)
    best = jnp.maximum(found[0], shifted).reshape(every)

    chosen = place[: 2 * rows, None] == order[None, :]
    ends = jnp.stack(
        [
            jnp.sum(jnp.where(chosen, best[None, :], 0.0), axis=1),
            jnp.sum(jnp.where(chosen, total[None, :], 0.0), axis=1),
        ]
    )
    ends = jnp.where(inner, ends[:, :rows], lax.ppermute(ends[:, rows:], "clus", IN_OUT))
    best, total = ends[0], ends[1]
    score = jnp.where(best > -2.0, D**0.5 * best, F32(-1.0))
    embedded = (unscaled.astype(F32) * lax.rsqrt(total + EPS)[:, None]).astype(BF16)
    return (embedded, score)


def solution(mesh):
    size = mesh.shape
    four = size["clus"] == 4 and size["groups"] == size["tp"] == size["rep"] == 2
    return jax.shard_map(
        line_of_four if four else any_mesh,
        mesh=mesh,
        in_specs=(
            P(("groups", "clus"), ("tp", "rep")),
            P(("groups", "clus"), ("tp", "rep")),
            P(("tp", "rep"), "clus"),
            P(("tp", "rep")),
            P(("groups", "clus"), None),
        ),
        out_specs=(P(("groups", "clus"), ("tp", "rep")), P(("groups", "clus"))),
        check_vma=False,
    )
```

```python
import jax
import jax.numpy as jnp
from jax import lax
from jax.experimental import pallas as pl
from jax.experimental.pallas import tpu as pltpu
from jax.sharding import PartitionSpec as P

D = 4096
CL_OWN = 6
EPS = 1e-06
F32, BF16 = jnp.float32, jnp.bfloat16


def best_match(block, valid):
    slots = block.shape[2]
    row_index = jnp.arange(block.shape[1], dtype=jnp.int32)
    col_index = jnp.arange(slots, dtype=jnp.int32)
    keep = valid[:, None, :] & (row_index[:, None] != col_index[None, :])[None, :, :]
    best = jnp.max(jnp.where(keep, block, jnp.float32(-4.0)), axis=2)
    found = jnp.any(keep, axis=2)
    return jnp.where(found, D**0.5 * best, jnp.float32(-1.0))


def any_mesh(hidden, residual, down_weight, norm_gain, cluster_id):
    rows = hidden.shape[0]
    owners = lax.axis_size("clus")
    per_owner = CL_OWN
    clusters = per_owner * owners
    capacity = 2 * rows // clusters
    span = owners * capacity
    terms = jnp.dot(
        hidden,
        lax.all_gather(down_weight, "clus", axis=1, tiled=True),
        preferred_element_type=jnp.float32,
    )
    summed = lax.psum_scatter(
        terms.astype(jnp.bfloat16), ("tp", "rep"), scatter_dimension=1, tiled=True
    ).astype(jnp.float32)
    scaled = (summed + residual.astype(jnp.float32)) * norm_gain[None, :]
    total = lax.psum(jnp.sum(scaled * scaled, axis=1), ("tp", "rep"))
    embedded = (scaled * lax.rsqrt(total + EPS)[:, None]).astype(jnp.bfloat16)
    labels = cluster_id[:, 0]
    owner = labels // per_owner
    local = labels % per_owner
    positions = jnp.arange(rows, dtype=jnp.int32)
    earlier = (labels[:, None] == labels[None, :]) & (positions[None, :] < positions[:, None])
    rank = jnp.sum(earlier.astype(jnp.int32), axis=1)
    target = local * span + owner * capacity + rank
    placing = jnp.arange(per_owner * span, dtype=jnp.int32)[:, None] == target[None, :]
    outgoing = jnp.dot(
        placing.astype(jnp.bfloat16), embedded, preferred_element_type=jnp.float32
    ).astype(jnp.bfloat16)
    outgoing = outgoing.reshape(per_owner, span, embedded.shape[1])
    present = (
        jnp.sum(placing.astype(jnp.float32), axis=1).astype(jnp.bfloat16).reshape(per_owner, span)
    )
    arrived, filled = (
        lax.all_to_all(outgoing, "clus", split_axis=1, concat_axis=1, tiled=True),
        lax.all_to_all(present, "clus", split_axis=1, concat_axis=1, tiled=True),
    )
    partial_value = jnp.einsum("ksd,ktd->kst", arrived, arrived, preferred_element_type=jnp.float32)
    valid = filled > 0
    gram = lax.psum(partial_value.astype(jnp.bfloat16), ("tp", "rep")).astype(jnp.float32)
    best = best_match(gram, valid)
    returned = lax.all_to_all(best, "clus", split_axis=1, concat_axis=1, tiled=True)
    score = jnp.sum(jnp.where(placing, returned.reshape(-1)[:, None], jnp.float32(0.0)), axis=0)
    return (embedded, score)


OUT_IN = [(0, 1), (3, 2)]
IN_OUT = [(1, 0), (2, 3)]
IN_IN = [(1, 2), (2, 1)]
FAR_IN = [(0, 2), (3, 1)]
SWAP = [(0, 1), (1, 0)]
CHUNKS = 4


def after(value, *earlier):
    return lax.optimization_barrier((value, *earlier))[0] if earlier else value


def zc(pairs):
    return [(a * 2 + b, c * 2 + d) for (a, b), (c, d) in pairs]


FREE = pl.CostEstimate(flops=1024, bytes_accessed=1024, transcendentals=0)


def late_part(y, rows, own, other, which=0):
    every, depth = rows.shape
    cols = other.shape[1]
    block = every // 2

    def body(_, a, b, own, other, out):
        total = jnp.dot(a[...], own[...], preferred_element_type=F32)
        total = total + jnp.dot(b[...], other[...], preferred_element_type=F32)
        out[...] = total.astype(BF16)

    return pl.pallas_call(
        body,
        grid_spec=pltpu.PrefetchScalarGridSpec(
            num_scalar_prefetch=1,
            grid=(every // block,),
            in_specs=[
                pl.BlockSpec((block, depth // 2), lambda i, y: (i, y[0])),
                pl.BlockSpec((block, depth // 2), lambda i, y: (i, 1 - y[0])),
                pl.BlockSpec((depth // 2, cols), lambda i, y: (0, which)),
                pl.BlockSpec((depth // 2, cols), lambda i, y: (0, 0)),
            ],
            out_specs=pl.BlockSpec((block, cols), lambda i, y: (i, 0)),
        ),
        out_shape=jax.ShapeDtypeStruct((every, cols), BF16),
        compiler_params=pltpu.CompilerParams(vmem_limit_bytes=24 * 2**20),
        cost_estimate=FREE,
        name="late_part",
    )(jnp.asarray(y, jnp.int32).reshape(1), rows, rows, own, other)


def product(rows, w):
    m, depth = rows.shape
    cols = w.shape[1]
    block = 256

    def body(a, b, out):
        out[...] = jnp.dot(a[...], b[...], preferred_element_type=F32).astype(BF16)

    return pl.pallas_call(
        body,
        grid=(cols // block,),
        in_specs=[
            pl.BlockSpec((m, depth), lambda i: (0, 0)),
            pl.BlockSpec((depth, block), lambda i: (0, i)),
        ],
        out_specs=pl.BlockSpec((m, block), lambda i: (0, i)),
        out_shape=jax.ShapeDtypeStruct((m, cols), BF16),
        compiler_params=pltpu.CompilerParams(vmem_limit_bytes=24 * 2**20),
        cost_estimate=FREE,
        name="product",
    )(rows, w)


def fold(x, part, met):
    rows, cols = part.shape
    width = cols // 2
    block = 384

    def body(_, a, b, c, d, keep, give):
        keep[...] = a[...].astype(F32) + b[...].astype(F32)
        give[...] = (c[...].astype(F32) + d[...].astype(F32)).astype(BF16)

    kept = pl.BlockSpec((block, width), lambda i, x: (i, x[0]))
    given = pl.BlockSpec((block, width), lambda i, x: (i, 1 - x[0]))
    out = pl.BlockSpec((block, width), lambda i, x: (i, 0))
    return pl.pallas_call(
        body,
        grid_spec=pltpu.PrefetchScalarGridSpec(
            num_scalar_prefetch=1,
            grid=(rows // block,),
            in_specs=[kept, kept, given, given],
            out_specs=[out, out],
        ),
        out_shape=[
            jax.ShapeDtypeStruct((rows, width), F32),
            jax.ShapeDtypeStruct((rows, width), BF16),
        ],
        compiler_params=pltpu.CompilerParams(vmem_limit_bytes=24 * 2**20),
        cost_estimate=FREE,
        name="fold",
    )(jnp.asarray(x, jnp.int32).reshape(1), part, met, part, met)


def tile_gram(is_late, place, late, early):
    every, width = late.shape
    tile = 128
    tiles = every // tile

    def body(flag, place, late, early, gram, squares, rows):
        rows[every:, :] = jnp.zeros((tile, width), BF16)
        value = jnp.where(flag[0] == 1, late[...], early[...])
        at = jax.lax.broadcasted_iota(jnp.int32, (tile, every), 0)
        for t in range(tiles):
            one = (at + t * tile == place[...]).astype(F32).astype(BF16)
            rows[t * tile : (t + 1) * tile, :] = jnp.dot(
                one, value, preferred_element_type=F32
            ).astype(BF16)
        i = jax.lax.broadcasted_iota(jnp.int32, (tile, tile), 0)
        j = jax.lax.broadcasted_iota(jnp.int32, (tile, tile), 1)
        for t in range(tiles):
            product = jax.lax.dot_general(
                rows[t * tile : (t + 1) * tile, :],
                rows[t * tile : (t + 2) * tile, :],
                (((1,), (1,)), ((), ())),
                preferred_element_type=F32,
            )
            gram[t] = product.astype(BF16)
            squares[t : t + 1, :] = jnp.sum(
                jnp.where(i == j, product[:, :tile], 0.0), axis=0, keepdims=True
            )

    return pl.pallas_call(
        body,
        grid_spec=pltpu.PrefetchScalarGridSpec(
            num_scalar_prefetch=1,
            grid=(1,),
            in_specs=[
                pl.BlockSpec((1, every), lambda i, f: (0, 0)),
                pl.BlockSpec((every, width), lambda i, f: (0, 0)),
                pl.BlockSpec((every, width), lambda i, f: (0, 0)),
            ],
            out_specs=[
                pl.BlockSpec((tiles, tile, 2 * tile), lambda i, f: (0, 0, 0)),
                pl.BlockSpec((tiles, tile), lambda i, f: (0, 0)),
            ],
            scratch_shapes=[pltpu.VMEM((every + tile, width), BF16)],
        ),
        out_shape=[
            jax.ShapeDtypeStruct((tiles, tile, 2 * tile), BF16),
            jax.ShapeDtypeStruct((tiles, tile), F32),
        ],
        compiler_params=pltpu.CompilerParams(vmem_limit_bytes=24 * 2**20),
        cost_estimate=FREE,
        name="tile_gram",
    )(jnp.asarray(is_late, jnp.int32).reshape(1), place.reshape(1, every), late, early)


def line_of_four(hidden, residual, down_weight, norm_gain, cluster_id):
    rows, depth = hidden.shape
    cols = down_weight.shape[1]
    half = cols // 2
    q = half // CHUNKS
    every = 4 * rows
    y, z, x, c = (lax.axis_index(a) for a in ("groups", "clus", "tp", "rep"))
    side = z // 2
    inner = (z == 1) | (z == 2)

    early_core = zc([((1, 0), (1, 1)), ((2, 1), (2, 0))])
    late_core = zc([((1, 1), (1, 0)), ((2, 0), (2, 1))])
    early_x = [(5, 7), (7, 5), (8, 10), (10, 8)]
    late_x = [(4, 6), (6, 4), (9, 11), (11, 9)]

    def over_rep(part, pairs):
        return fold(x, part, lax.ppermute(part, ("clus", "rep"), pairs))

    def over_tp(keep, give, pairs):
        return keep + lax.ppermute(give, ("clus", "tp", "rep"), pairs).astype(F32)

    def across(value, *gates):
        return lax.ppermute(after(value, *gates), "groups", SWAP)

    def inward(value, *gates):
        return lax.ppermute(after(value, *gates), "clus", OUT_IN)

    stage = lax.optimization_barrier
    names = cluster_id[:, 0]
    h_outer = inward(hidden)
    h_other = lax.ppermute(hidden, "clus", IN_IN)
    names = jnp.concatenate(
        [names] + [lax.ppermute(names, "clus", pairs) for pairs in (OUT_IN, IN_IN, FAR_IN)]
    )
    mine = lax.dynamic_slice_in_dim(residual, x * half, half, 1)
    theirs = lax.dynamic_slice_in_dim(residual, (1 - x) * half, half, 1)
    w_half = lax.dynamic_slice_in_dim(down_weight, y * (depth // 2), depth // 2, 0)
    taken = lambda j, n: [w_half[:, i * half + j * q : i * half + (j + n) * q] for i in range(2)]
    pieces = [jnp.concatenate(v, axis=1) for v in (taken(0, 2), taken(2, 2))]
    part = product(hidden, down_weight)

    h_outer, h_other, names, part, pieces, theirs = stage(
        (h_outer, h_other, names, part, pieces, theirs)
    )
    got0 = inward(pieces[0])
    top = rows // 2
    far0 = lax.ppermute(h_outer[:top], "clus", IN_IN)
    came = lax.ppermute(theirs, "tp", SWAP)
    gain_other = lax.ppermute(norm_gain, "tp", SWAP)
    first = []
    part = [part] + [product(after(v, came), down_weight) for v in (h_outer, h_other)]
    first += [over_rep(v, early_core) for v in part]

    got0, pieces, came, gain_other, part, names, far0, first = stage(
        (got0, pieces, came, gain_other, part, names, far0, first)
    )
    far1 = lax.ppermute(h_outer[top:], "clus", IN_IN)
    got1 = inward(pieces[1])
    other0 = across(got0)
    order = jnp.arange(every, dtype=jnp.int32)
    planes = jnp.where(side == 0, jnp.array([1, 0, 2, 3]), jnp.array([2, 3, 1, 0]))
    ids = (planes[:, None] * rows + order[None, :rows]).reshape(every)
    before = (names[None, :] < names[:, None]) | (
        (names[None, :] == names[:, None]) & (ids[None, :] < ids[:, None])
    )
    place = jnp.sum(before.astype(jnp.int32), axis=1)
    at_place = order[:, None] == place[None, :]
    sorted_labels = jnp.sum(jnp.where(at_place, names[None, :], 0), axis=1)
    near_side = jnp.where(side == x, mine, came)
    far_side = jnp.where(side == x, came, mine)

    got1, other0, far0, far1, place, sorted_labels, first, near_side, far_side = stage(
        (got1, other0, far0, far1, place, sorted_labels, first, near_side, far_side)
    )
    far = jnp.concatenate([far0, far1], axis=0)
    other1 = across(got1)
    stack = jnp.concatenate([hidden, h_outer, h_other, far], axis=0)
    late0 = late_part(y, stack, got0, other0)
    res_near = inward(near_side)
    res_far = lax.ppermute(far_side, "clus", FAR_IN)
    res_other = lax.ppermute(after(far_side, late0), "clus", IN_IN)
    res = jnp.concatenate([near_side, res_near, res_other, res_far], axis=0).astype(F32)
    first = over_tp(*(jnp.concatenate(v, axis=0) for v in zip(*first)), early_x)
    last = over_rep(product(after(far, late0), down_weight), early_core)
    sum0 = over_rep(late0, late_core)
    late1 = late_part(y, after(stack, *last), got1, other1)
    last = over_tp(*last, early_x)
    sum0 = over_tp(*sum0, late_x)
    sum1 = over_tp(*over_rep(late1, late_core), late_x)
    early = jnp.concatenate([first, last], axis=0)

    gain_late = jnp.where(x == c, norm_gain, gain_other)
    gain_early = jnp.where(x == c, gain_other, norm_gain)
    gain_late = lax.dynamic_slice_in_dim(gain_late, x * half, half, 0)[None, :]
    gain_early = lax.dynamic_slice_in_dim(gain_early, x * half, half, 0)[None, :]
    early = ((early + res) * gain_early).astype(BF16)
    def home(value, near, other, far, where):
        value = value.reshape(4, rows, half)
        moved = (
            lax.ppermute(value[1], ("clus", "rep"), zc(near))
            + lax.ppermute(value[2], ("clus", "rep"), zc(other))
            + lax.ppermute(value[3], ("clus", "rep"), zc(far))
        )
        return jnp.where(z == where, value[0], moved)

    early_rows = home(
        early,
        [((2, 0), (3, 0)), ((1, 1), (0, 1))],
        [((2, 0), (1, 0)), ((1, 1), (2, 1))],
        [((2, 0), (0, 0)), ((1, 1), (3, 1))],
        2 - c,
    )
    sum1 = after(sum1, early_rows)
    late = [
        ((v + res[:, j * q : k * q]) * gain_late[:, j * q : k * q]).astype(BF16)
        for v, j, k in ((sum0, 0, 2), (sum1, 2, 4))
    ]
    late = jnp.concatenate(late, axis=1)

    tile = 128
    tiles = every // tile
    gram, squares = tile_gram(z == 1 + c, place, late, early)
    gram = gram.reshape(every, 2 * tile)
    squares = squares.reshape(tiles // 2, 2 * tile)
    spare = -tiles % 16

    def pack(gram, squares):
        high = lax.reduce_precision(squares, 8, 7)
        ends = jnp.zeros((spare, 2 * tile), BF16)
        return jnp.concatenate(
            [gram.astype(BF16), high.astype(BF16), (squares - high).astype(BF16), ends], axis=0
        )

    def meet(gram, squares, met):
        n = gram.shape[0]
        ends = met[n : n + tiles].astype(F32)
        return (
            gram.astype(F32) + met[:n].astype(F32),
            squares + ends[: tiles // 2] + ends[tiles // 2 :],
        )

    for axis, index in (("rep", c), ("tp", x)):
        n = gram.shape[0] // 2
        give = lax.dynamic_slice_in_dim(gram, (1 - index) * n, n, 0)
        keep = lax.dynamic_slice_in_dim(gram, index * n, n, 0)
        gram, squares = meet(keep, squares, lax.ppermute(pack(give, squares), axis, SWAP))
    late_rows = home(
        late,
        [((1, 0), (0, 0)), ((2, 1), (3, 1))],
        [((1, 0), (2, 0)), ((2, 1), (1, 1))],
        [((1, 0), (3, 0)), ((2, 1), (0, 1))],
        1 + c,
    )
    kept = jnp.where(x == c, late_rows, early_rows)
    came = lax.ppermute(late_rows, ("tp", "rep"), [(2, 0), (1, 3)]) + lax.ppermute(
        early_rows, ("tp", "rep"), [(0, 2), (3, 1)]
    )
    unscaled = jnp.where(
        x == 0, jnp.concatenate([kept, came], axis=1), jnp.concatenate([came, kept], axis=1)
    )

    gram = after(gram, late_rows)
    gram = gram.astype(BF16)
    gram, squares = meet(gram, squares, lax.ppermute(pack(gram, squares), "clus", IN_IN))
    gram = gram.reshape(-1, tile, 2 * tile)
    total = squares.reshape(every)

    n = tiles // 4
    first = (2 * c + x) * n
    pad = lambda a, v: jnp.concatenate([a, jnp.full((tile,), v, a.dtype)]).reshape(tiles + 1, tile)
    span = lambda a: lax.dynamic_slice_in_dim(a, first, n + 1, 0)
    both = lambda a: jnp.concatenate([a[:-1], a[1:]], axis=1)
    scale = span(pad(lax.rsqrt(total + EPS), 0.0))
    tags = span(pad(sorted_labels, -1))
    sims = gram * scale[:-1, :, None] * both(scale)[:, None, :]
    at = jnp.arange(tile, dtype=jnp.int32)[:, None] != jnp.arange(2 * tile, dtype=jnp.int32)[None, :]
    keep = (tags[:-1, :, None] == both(tags)[:, None, :]) & at[None]
    sims = jnp.where(keep, sims, F32(-4.0))
    found = jnp.stack([jnp.max(sims, axis=2), jnp.max(sims[:, :, tile:], axis=1)])
    for axis, index in (("tp", x), ("rep", c)):
        met = lax.ppermute(found, axis, SWAP)
        found = jnp.where(
            index == 0, jnp.concatenate([found, met], axis=1), jnp.concatenate([met, found], axis=1)
        )
    shifted = jnp.concatenate([jnp.full((1, tile), -4.0, F32), found[1, :-1]], axis=0)
    best = jnp.maximum(found[0], shifted).reshape(every)

    chosen = place[: 2 * rows, None] == order[None, :]
    ends = jnp.stack(
        [
            jnp.sum(jnp.where(chosen, best[None, :], 0.0), axis=1),
            jnp.sum(jnp.where(chosen, total[None, :], 0.0), axis=1),
        ]
    )
    ends = jnp.where(inner, ends[:, :rows], lax.ppermute(ends[:, rows:], "clus", IN_OUT))
    best, total = ends[0], ends[1]
    score = jnp.where(best > -2.0, D**0.5 * best, F32(-1.0))
    embedded = (unscaled.astype(F32) * lax.rsqrt(total + EPS)[:, None]).astype(BF16)
    return (embedded, score)


def solution(mesh):
    size = mesh.shape
    four = size["clus"] == 4 and size["groups"] == size["tp"] == size["rep"] == 2
    return jax.shard_map(
        line_of_four if four else any_mesh,
        mesh=mesh,
        in_specs=(
            P(("groups", "clus"), ("tp", "rep")),
            P(("groups", "clus"), ("tp", "rep")),
            P(("tp", "rep"), "clus"),
            P(("tp", "rep")),
            P(("groups", "clus"), None),
        ),
        out_specs=(P(("groups", "clus"), ("tp", "rep")), P(("groups", "clus"))),
        check_vma=False,
    )
```
